512 devices in a mesh: dp: 4 (over x), trow: 16 (over y_lo, z), tcol: 8 (over y_hi, core).
Axes of the slice: x: 4, y: 8 (y_hi: 4, y_lo: 2; y = y_hi * 2 + y_lo), z: 8, core: 2. Of those that a mesh axis runs over, the one named last changes fastest.
Arguments:
- gate: bfloat16 [4, 16384, 256], P('dp', ('trow', 'tcol')), may hold values from -6 to 6
- value: bfloat16 [4, 16384, 256], P('dp', ('trow', 'tcol')), may hold values from -6 to 6
- grad_out: bfloat16 [4, 16384, 256], P('dp', ('trow', 'tcol')), may hold values from -6 to 6
- filter_raw: float32 [16384, 256], P(('trow', 'tcol')), may hold values from -6 to 6
Outputs:
- grad_gate: bfloat16 [4, 16384, 256], P('dp', ('trow', 'tcol'))
- grad_value: bfloat16 [4, 16384, 256], P('dp', ('trow', 'tcol'))
- grad_filter: float32 [16384, 256], P(('trow', 'tcol'), 'dp')
The draws below stay inside these ranges and needn't reach their ends.
All inputs are finite; a program needn't handle non-finite values.
Results may differ from the reference program's by a relative error of at most 0.001.
Values sent between devices are 32-bit elements; how exact they have to be, the bound alone decides.
A program may use at most 64 MiB of HBM per device.

```python
import jax
import jax.numpy as jnp
from jax import lax

D = 256
NSEQ = 4
SEQLEN = 16384


def block_levels(rng, extent, shards, low, high):
    factor_of, own = 1.0, jax.random.fold_in(rng, 6)
    for axis_at, shards_of in shards:
        steps = jnp.exp(jax.random.uniform(jax.random.fold_in(own, axis_at), (shards_of,), jnp.float32, low / len(shards), high / len(shards)))
        factor_of = factor_of * jnp.repeat(steps, extent[axis_at] // shards_of).reshape([-1 if axis == axis_at else 1 for axis in range(len(extent))])
    return factor_of


def scatter_about(stream_key, dims, spread, bound, cuts=(), dtype=jnp.bfloat16):
    drawn = jax.random.normal(stream_key, dims, jnp.float32) * spread
    if len(cuts) > 0:
        drawn = block_levels(stream_key, dims, cuts, -0.22, 0.18) * drawn
    return jnp.clip(drawn, min=-bound, max=bound).astype(dtype)


def setup_inputs(seed: int = 0) -> dict:
    arg_keys = jax.random.split(jax.random.key(seed), 5)
    gate = scatter_about(arg_keys[0], (NSEQ, SEQLEN, D), 1.0, 6.0, ((0, 4), (1, 128)))
    value = scatter_about(arg_keys[1], (NSEQ, SEQLEN, D), 1.0, 6.0, ((0, 4), (1, 128)))
    grad_out = scatter_about(arg_keys[2], (NSEQ, SEQLEN, D), 1.0, 6.0, ((0, 4), (1, 128)))
    filter_raw = scatter_about(arg_keys[3], (SEQLEN, D), 1.0, 6.0, ((0, 128),), jnp.float32)
    return dict(gate=gate, value=value, grad_out=grad_out, filter_raw=filter_raw)


def reference(gate, value, grad_out, filter_raw):
    total = 2 * SEQLEN
    scale = SEQLEN ** -0.5
    filt = filter_raw.astype(jnp.float32) * scale
    filt_spec = jnp.fft.rfft(filt, n=total, axis=0)

    def one_sequence(inputs):
        gate_seq, value_seq, grad_seq = inputs
        value_f = value_seq.astype(jnp.float32)
        grad_f = grad_seq.astype(jnp.float32)
        value_spec = jnp.fft.rfft(value_f, n=total, axis=0)
        conv = jnp.fft.irfft(value_spec * filt_spec, n=total, axis=0)[:SEQLEN]
        grad_gate = (grad_f * conv).astype(jnp.bfloat16)
        grad_conv = grad_f * gate_seq.astype(jnp.float32)
        grad_spec = jnp.fft.rfft(grad_conv, n=total, axis=0)
        grad_value = jnp.fft.irfft(grad_spec * jnp.conj(filt_spec), n=total, axis=0)[:SEQLEN]
        corr = jnp.fft.irfft(grad_spec * jnp.conj(value_spec), n=total, axis=0)[:SEQLEN]
        return grad_gate, grad_value.astype(jnp.bfloat16), corr

    grad_gate, grad_value, corr = lax.map(one_sequence, (gate, value, grad_out))
    grad_filter = jnp.sum(corr, axis=0) * scale
    return grad_gate, grad_value, grad_filter.astype(jnp.float32)
```

```python
import jax
import jax.numpy as jnp
import ml_dtypes
import numpy as np
from jax import lax
from jax.experimental import pallas as pl
from jax.experimental.pallas import tpu as pltpu
from jax.sharding import PartitionSpec as P

MESH = pl.DeviceIdType.MESH
LANES = 128
F32 = jnp.float32
BF16 = jnp.bfloat16


def row_of(trow, tcol):
    y_lo, z = trow // 8, trow % 8
    return (z % 4) * 32 + (y_lo * 2 + z // 4) * 8 + tcol


def split_const(matrix):
    high = matrix.astype(np.float32).astype(ml_dtypes.bfloat16)
    low = (matrix - high.astype(np.float64)).astype(np.float32).astype(ml_dtypes.bfloat16)
    return high, low


def constants():
    block = np.zeros(LANES, np.int64)
    for trow in range(16):
        for tcol in range(8):
            block[row_of(trow, tcol)] = trow * 8 + tcol
    odd = 2 * np.arange(LANES) + 1
    theta = 2 * np.pi * ((odd[:, None] * block[None, :]) % 512) / 512
    wide = np.zeros((2, 2, LANES, LANES, 2))
    for half in range(2):
        wide[0, half, :, :, half] = np.cos(theta)
        wide[1, half, :, :, half] = -np.sin(theta)
    outer = wide.reshape(4 * LANES, 2 * LANES)
    place = np.arange(LANES)
    angle = 2 * np.pi * ((place[:, None] * place[None, :]) % LANES) / LANES
    cos, sin = np.cos(angle), np.sin(angle)
    inner = np.block([[cos, -sin], [sin, cos]])
    back = np.block([[cos, sin], [-sin, cos]])
    phi = 2 * np.pi * (odd[:, None] * place[None, :]) / 65536
    scale = 2.0 ** -21
    return (
        np.stack(split_const(outer)),
        np.stack(split_const(inner) + split_const(back)),
        np.stack(split_const(outer.T * scale)),
        np.stack([np.cos(phi), np.sin(phi)]).astype(np.float32),
    )


def halves(x):
    high = x.astype(BF16)
    low = (x - high.astype(F32)).astype(BF16)
    return high, low


def dot(a, b):
    return jnp.dot(a, b, preferred_element_type=F32)


def outer_dot(mat_high, mat_low, x):
    high, low = halves(x)
    both = dot(mat_high, jnp.concatenate([high, low], axis=1))
    return both[:, :LANES] + both[:, LANES:] + dot(mat_low, high)


def inner_dot(x, mat_high, mat_low):
    high, low = halves(x)
    return dot(high, mat_high) + dot(low, mat_high) + dot(high, mat_low)


def turn(real, imag, cos, sin):
    shape = (2, LANES, LANES)
    real, imag = real.reshape(shape), imag.reshape(shape)
    out_real = real * cos - imag * sin
    out_imag = imag * cos + real * sin
    return out_real.reshape(2 * LANES, LANES), out_imag.reshape(2 * LANES, LANES)


def kernel(
    value_hbm, gate_hbm, grad_hbm, filt_hbm, outer_hbm, inner_hbm, last_hbm, twid_hbm,
    gate_out, value_out, filt_out,
    value_in, gate_in, grad_in, filt_in, outer, inner, last, twid,
    value_send, filt_send,
    grad_send, value_col, grad_col, filt_col,
    conv_col, back_col, corr_col, conv_row, back_row,
    corr_parts, corr_sum, load_sem, send_sem, recv_sem,
):
    seq = lax.axis_index("dp")
    trow = lax.axis_index("trow")
    tcol = lax.axis_index("tcol")
    me = trow * 8 + tcol
    my_row = row_of(trow, tcol)

    loads = [
        pltpu.make_async_copy(src, dst, load_sem.at[i])
        for i, (src, dst) in enumerate(
            (
                (filt_hbm, filt_in),
                (value_hbm, value_in),
                (grad_hbm, grad_in),
                (gate_hbm, gate_in),
                (outer_hbm, outer),
                (inner_hbm, inner),
                (twid_hbm, twid),
                (last_hbm, last),
            )
        )
    ]
    for load in loads:
        load.start()

    barrier = pltpu.get_barrier_semaphore()

    def greet(k, carry):
        peer = me ^ k
        pl.semaphore_signal(
            barrier, inc=1, device_id=(seq, peer // 8, peer % 8), device_id_type=MESH
        )
        return carry

    lax.fori_loop(1, LANES, greet, 0)
    for k in range(1, 4):
        pl.semaphore_signal(
            barrier, inc=1, device_id=(seq ^ k, trow, tcol), device_id_type=MESH
        )

    def spread(rows, out):
        turned = rows.T
        out[pl.ds(0, LANES, stride=2), :] = turned[:LANES]
        out[pl.ds(1, LANES, stride=2), :] = turned[LANES:]

    loads[0].wait()
    spread(filt_in[...], filt_send)
    loads[1].wait()
    spread(value_in[...].astype(F32), value_send)
    loads[2].wait()
    loads[3].wait()
    spread(grad_in[...].astype(F32) * gate_in[...].astype(F32), grad_send)

    pl.semaphore_wait(barrier, LANES - 1 + 3)

    def pair(ref, row):
        return ref.at[pl.ds(pl.multiple_of(row * 2, 2), 2)]

    def to_columns(src, dst, at):
        def send(k, carry):
            peer = me ^ k
            pltpu.make_async_remote_copy(
                pair(src, peer), pair(dst, my_row), send_sem.at[at], recv_sem.at[at],
                device_id=(seq, peer // 8, peer % 8), device_id_type=MESH,
            ).start()
            return carry

        pltpu.make_async_copy(pair(src, me), pair(dst, my_row), recv_sem.at[at]).start()
        lax.fori_loop(1, LANES, send, 0)

    def to_rows(src, dst, at):
        def send(k, carry):
            peer = me ^ k
            peer_row, peer_col = peer // 8, peer % 8
            pltpu.make_async_remote_copy(
                pair(src, row_of(peer_row, peer_col)), pair(dst, me), send_sem.at[at], recv_sem.at[at],
                device_id=(seq, peer_row, peer_col), device_id_type=MESH,
            ).start()
            return carry

        pltpu.make_async_copy(pair(src, my_row), pair(dst, me), recv_sem.at[at]).start()
        lax.fori_loop(1, LANES, send, 0)

    def take(view, sem):
        pltpu.make_async_copy(view, view, sem).wait()

    quarter = 2 * LANES // 4
    my_turn = trow % 4 == seq

    @pl.when(my_turn)
    def _():
        to_columns(filt_send, filt_col, 0)

    to_columns(value_send, value_col, 1)
    to_columns(grad_send, grad_col, 2)

    def forward(column):
        spec = outer_dot(outer[0], outer[1], column)
        real, imag = turn(spec[: 2 * LANES], spec[2 * LANES :], twid[0], -twid[1])
        spec = inner_dot(jnp.concatenate([real, imag], axis=1), inner[0], inner[1])
        return spec[:, :LANES], spec[:, LANES:]

    def inverse(real, imag):
        spec = inner_dot(jnp.concatenate([real, imag], axis=1), inner[2], inner[3])
        real, imag = turn(spec[:, :LANES], spec[:, LANES:], twid[0], twid[1])
        return outer_dot(last[0], last[1], jnp.concatenate([real, imag], axis=0))

    mine = filt_col.at[pl.ds(pl.multiple_of(seq * quarter, quarter), quarter)]
    take(mine, recv_sem.at[0])
    for k in range(1, 4):
        pltpu.make_async_remote_copy(
            mine, mine, send_sem.at[3], recv_sem.at[3],
            device_id=(seq ^ k, trow, tcol), device_id_type=MESH,
        ).start()

    for load in loads[4:]:
        load.wait()
    take(value_col, recv_sem.at[1])
    value_real, value_imag = forward(value_col[...])
    take(filt_col.at[pl.ds(0, 3 * quarter)], recv_sem.at[3])
    filt_real, filt_imag = forward(filt_col[...])
    conv_col[...] = inverse(
        value_real * filt_real - value_imag * filt_imag,
        value_real * filt_imag + value_imag * filt_real,
    )
    to_rows(conv_col, conv_row, 4)

    take(grad_col, recv_sem.at[2])
    grad_real, grad_imag = forward(grad_col[...])
    corr = inverse(
        grad_real * value_real + grad_imag * value_imag,
        grad_imag * value_real - grad_real * value_imag,
    )
    corr_col[...] = corr
    for half in range(2):
        corr_parts[3 + half] = corr_col[pl.ds(half, LANES, stride=2), :]
    for half in range(2):
        owner = half * 2 + me // 64

        @pl.when(owner != seq)
        def _():
            pltpu.make_async_remote_copy(
                corr_parts.at[3 + half], corr_parts.at[(seq ^ owner) - 1], send_sem.at[6 + half], recv_sem.at[6],
                device_id=(owner, trow, tcol), device_id_type=MESH,
            ).start()

    back_col[...] = inverse(
        grad_real * filt_real + grad_imag * filt_imag,
        grad_imag * filt_real - grad_real * filt_imag,
    )
    to_rows(back_col, back_row, 5)

    own_half = seq // 2
    summing = me // 64 == seq % 2

    @pl.when(summing)
    def _():
        take(corr_parts.at[pl.ds(0, 3)], recv_sem.at[6])
        own = jnp.where(own_half == 0, corr_parts[3], corr_parts[4])
        corr_sum[...] = own + corr_parts[0] + corr_parts[1] + corr_parts[2]
        at = me % 64

        def send(k, carry):
            peer = me ^ k
            peer_row, peer_col = peer // 8, peer % 8
            pltpu.make_async_remote_copy(
                corr_sum.at[pl.ds(row_of(peer_row, peer_col), 1)], filt_out.at[pl.ds(at, 1)],
                send_sem.at[8], recv_sem.at[7],
                device_id=(seq, peer_row, peer_col), device_id_type=MESH,
            ).start()
            return carry

        pltpu.make_async_copy(
            corr_sum.at[pl.ds(my_row, 1)], filt_out.at[pl.ds(at, 1)], recv_sem.at[7]
        ).start()
        lax.fori_loop(1, LANES, send, 0)

    def gather(rows):
        return jnp.concatenate(
            [rows[pl.ds(0, LANES, stride=2), :].T, rows[pl.ds(1, LANES, stride=2), :].T], axis=1
        )

    take(conv_row, recv_sem.at[4])
    gate_out[...] = (grad_in[...].astype(F32) * gather(conv_row)).astype(BF16)
    take(back_row, recv_sem.at[5])
    value_out[...] = gather(back_row).astype(BF16)
    take(filt_out, recv_sem.at[7])

    most = pl.ds(0, 2 * LANES - 2)

    @pl.when(my_turn)
    def _():
        take(filt_send.at[most], send_sem.at[0])

    take(value_send.at[most], send_sem.at[1])
    take(grad_send.at[most], send_sem.at[2])
    take(filt_col.at[pl.ds(0, 3 * quarter)], send_sem.at[3])
    take(conv_col.at[most], send_sem.at[4])
    take(back_col.at[most], send_sem.at[5])
    for half in range(2):
        owner = half * 2 + me // 64

        @pl.when(owner != seq)
        def _():
            take(corr_parts.at[3 + half], send_sem.at[6 + half])

    @pl.when(summing)
    def _():
        take(corr_sum.at[pl.ds(0, LANES - 1)], send_sem.at[8])


def local(gate, value, grad_out, filter_raw):
    wide = pltpu.VMEM((2 * LANES, LANES), F32)
    bf16 = pltpu.VMEM((LANES, 2 * LANES), BF16)
    scratch = [
        bf16, bf16, bf16, pltpu.VMEM((LANES, 2 * LANES), F32),
        pltpu.VMEM((2, 4 * LANES, 2 * LANES), BF16),
        pltpu.VMEM((4, 2 * LANES, 2 * LANES), BF16),
        pltpu.VMEM((2, 2 * LANES, 4 * LANES), BF16),
        pltpu.VMEM((2, LANES, LANES), F32),
    ]
    scratch += [wide] * 11
    scratch += [
        pltpu.VMEM((5, LANES, LANES), F32),
        pltpu.VMEM((LANES, LANES), F32),
        pltpu.SemaphoreType.DMA((8,)),
        pltpu.SemaphoreType.DMA((9,)),
        pltpu.SemaphoreType.DMA((8,)),
    ]
    grad_gate, grad_value, grad_filter = pl.pallas_call(
        kernel,
        name="gated_conv_backward",
        out_shape=(
            jax.ShapeDtypeStruct((LANES, 2 * LANES), BF16),
            jax.ShapeDtypeStruct((LANES, 2 * LANES), BF16),
            jax.ShapeDtypeStruct((LANES // 2, LANES), F32),
        ),
        in_specs=[pl.BlockSpec(memory_space=pl.ANY)] * 8,
        out_specs=(pl.BlockSpec(memory_space=pltpu.VMEM),) * 3,
        scratch_shapes=scratch,
        compiler_params=pltpu.CompilerParams(
            collective_id=0, has_side_effects=True, vmem_limit_bytes=32 << 20
        ),
    )(value[0], gate[0], grad_out[0], filter_raw, *(jnp.asarray(c) for c in constants()))
    return grad_gate[None], grad_value[None], grad_filter.T


def solution(mesh):
    tokens = P("dp", ("trow", "tcol"), None)
    return jax.shard_map(
        local,
        mesh=mesh,
        in_specs=(tokens, tokens, tokens, P(("trow", "tcol"), None)),
        out_specs=(tokens, tokens, P(("trow", "tcol"), "dp")),
        check_vma=False,
    )
```

```python
import functools

import jax
import jax.numpy as jnp
import ml_dtypes
import numpy as np
from jax import lax
from jax.experimental import pallas as pl
from jax.experimental.pallas import tpu as pltpu
from jax.sharding import PartitionSpec as P

MESH = pl.DeviceIdType.MESH
LANES = 128
F32 = jnp.float32
BF16 = jnp.bfloat16


def row_of(trow, tcol):
    return ((trow & 3) << 5) | ((trow >> 2) << 3) | tcol


def split_const(matrix):
    high = matrix.astype(np.float32).astype(ml_dtypes.bfloat16)
    low = (matrix - high.astype(np.float64)).astype(np.float32).astype(ml_dtypes.bfloat16)
    return high, low


def constants():
    block = np.zeros(LANES, np.int64)
    for trow in range(16):
        for tcol in range(8):
            block[row_of(trow, tcol)] = trow * 8 + tcol
    odd = 2 * np.arange(LANES) + 1
    theta = 2 * np.pi * ((odd[:, None] * block[None, :]) % 512) / 512
    wide = np.zeros((2, 2, LANES, LANES, 2))
    for half in range(2):
        wide[0, half, :, :, half] = np.cos(theta)
        wide[1, half, :, :, half] = -np.sin(theta)
    outer = wide.reshape(4 * LANES, 2 * LANES)
    place = np.arange(LANES)
    angle = 2 * np.pi * ((place[:, None] * place[None, :]) % LANES) / LANES
    cos, sin = np.cos(angle), np.sin(angle)
    inner = np.block([[cos, -sin], [sin, cos]])
    back = np.block([[cos, sin], [-sin, cos]])
    phi = 2 * np.pi * (odd[:, None] * place[None, :]) / 65536
    scale = 2.0 ** -21
    return (
        np.stack(split_const(outer)),
        np.stack(split_const(inner) + split_const(back)),
        np.stack(split_const(outer.T * scale)),
        np.stack([np.cos(phi), np.sin(phi)]).astype(np.float32),
    )


def each_peer(trow, tcol, act):
    y, z, core = (tcol & 6) | (trow >> 3), trow & 7, tcol & 1

    def column(dz, own):
        peer_z = (z + dz) & 7
        for dy in (4, 3, 5, 2, 6, 1, 7, 0):
            peer_y = (y + dy) & 7
            peer_row, peer_col = ((peer_y & 1) << 3) | peer_z, (peer_y & 6) | core
            act(peer_row, peer_col ^ 1)
            if not (own and dy == 0):
                act(peer_row, peer_col)

    def step(t, carry):
        away = (t + 1) >> 1
        column(jnp.where((t & 1) == 1, 4 - away, 4 + away), False)
        return carry

    lax.fori_loop(0, 7, step, 0)
    column(0, True)


def each_peer_late(trow, tcol, act):
    y, z, core = (tcol & 6) | (trow >> 3), trow & 7, tcol & 1

    def step(t, carry):
        peer_z = ((z + 1 + t) & 3) | ((~t) & 4)
        for dy in (4, 3, 5, 2, 6, 1, 7, 0):
            peer_y = (y + dy) & 7
            peer_row, peer_col = ((peer_y & 1) << 3) | peer_z, (peer_y & 6) | core
            act(peer_row, peer_col ^ 1)
            if dy:
                act(peer_row, peer_col)
            else:
                pl.when(peer_z != z)(functools.partial(act, peer_row, peer_col))
        return carry

    lax.fori_loop(0, 8, step, 0)


def halves(x):
    high = x.astype(BF16)
    low = (x - high.astype(F32)).astype(BF16)
    return high, low


def dot(a, b):
    return jnp.dot(a, b, preferred_element_type=F32)


def outer_dot(mat_high, mat_low, x):
    high, low = halves(x)
    both = dot(mat_high, jnp.concatenate([high, low], axis=1))
    return both[:, :LANES] + both[:, LANES:] + dot(mat_low, high)


def inner_dot(x, mat_high, mat_low):
    high, low = halves(x)
    return dot(high, mat_high) + dot(low, mat_high) + dot(high, mat_low)


def turn(real, imag, cos, sin):
    shape = (2, LANES, LANES)
    real, imag = real.reshape(shape), imag.reshape(shape)
    out_real = real * cos - imag * sin
    out_imag = imag * cos + real * sin
    return out_real.reshape(2 * LANES, LANES), out_imag.reshape(2 * LANES, LANES)


def kernel(
    value_hbm, gate_hbm, grad_hbm, filt_hbm, outer_hbm, inner_hbm, last_hbm, twid_hbm,
    gate_out, value_out, filt_out,
    value_in, gate_in, grad_in, filt_in, outer, inner, last, twid,
    value_send, filt_send,
    grad_send, value_col, grad_col, filt_col,
    conv_col, back_col, corr_col, conv_row, back_row,
    corr_parts, corr_sum, load_sem, send_sem, recv_sem,
):
    seq = lax.axis_index("dp")
    trow = lax.axis_index("trow")
    tcol = lax.axis_index("tcol")
    me = trow * 8 + tcol
    my_row = row_of(trow, tcol)

    barrier = pltpu.get_barrier_semaphore()

    def greet(peer_row, peer_col):
        pl.semaphore_signal(
            barrier, inc=1, device_id=(seq, peer_row, peer_col), device_id_type=MESH
        )

    each_peer(trow, tcol, greet)
    for k in range(1, 4):
        pl.semaphore_signal(
            barrier, inc=1, device_id=(seq ^ k, trow, tcol), device_id_type=MESH
        )

    loads = [
        pltpu.make_async_copy(src, dst, load_sem.at[i])
        for i, (src, dst) in enumerate(
            (
                (filt_hbm, filt_in),
                (value_hbm, value_in),
                (grad_hbm, grad_in),
                (gate_hbm, gate_in),
                (outer_hbm, outer),
                (inner_hbm, inner),
                (twid_hbm, twid),
                (last_hbm, last),
            )
        )
    ]
    for load in loads:
        load.start()

    def spread(rows, out):
        turned = rows.T
        out[pl.ds(0, LANES, stride=2), :] = turned[:LANES]
        out[pl.ds(1, LANES, stride=2), :] = turned[LANES:]

    loads[0].wait()
    spread(filt_in[...], filt_send)
    loads[1].wait()
    spread(value_in[...].astype(F32), value_send)
    loads[2].wait()
    loads[3].wait()
    spread(grad_in[...].astype(F32) * gate_in[...].astype(F32), grad_send)

    pl.semaphore_wait(barrier, LANES - 1 + 3)

    def pair(ref, row):
        return ref.at[pl.ds(pl.multiple_of(row * 2, 2), 2)]

    def to_columns(src, dst, at):
        there = pair(dst, my_row)

        def send(peer_row, peer_col):
            pltpu.make_async_remote_copy(
                pair(src, peer_row * 8 + peer_col), there, send_sem.at[at], recv_sem.at[at],
                device_id=(seq, peer_row, peer_col), device_id_type=MESH,
            ).start()

        pltpu.make_async_copy(pair(src, me), there, recv_sem.at[at]).start()
        each_peer_late(trow, tcol, send)

    def to_rows(src, dst, at):
        there = pair(dst, me)

        def send(peer_row, peer_col):
            pltpu.make_async_remote_copy(
                pair(src, row_of(peer_row, peer_col)), there, send_sem.at[at], recv_sem.at[at],
                device_id=(seq, peer_row, peer_col), device_id_type=MESH,
            ).start()

        pltpu.make_async_copy(pair(src, my_row), there, recv_sem.at[at]).start()
        each_peer(trow, tcol, send)

    def take(view, sem):
        pltpu.make_async_copy(view, view, sem).wait()

    quarter = 2 * LANES // 4

    filt_there = pair(filt_col, my_row)

    def send_filt(peer_row, peer_col):
        pltpu.make_async_remote_copy(
            pair(filt_send, peer_row * 8 + peer_col), filt_there, send_sem.at[0], recv_sem.at[0],
            device_id=(seq, peer_row, peer_col), device_id_type=MESH,
        ).start()

    for high in (4, 0):
        peer_z = ((trow ^ seq) & 3) | high
        for y_lo in (8, 0):
            for j in range(7, -1, -1):
                peer_row, peer_col = ((trow & 8) ^ y_lo) | peer_z, tcol ^ j
                if y_lo or j:
                    send_filt(peer_row, peer_col)
                else:
                    pl.when(peer_row != trow)(functools.partial(send_filt, peer_row, peer_col))

    @pl.when(seq == 0)
    def _():
        pltpu.make_async_copy(pair(filt_send, me), filt_there, recv_sem.at[0]).start()

    to_columns(value_send, value_col, 1)
    to_columns(grad_send, grad_col, 2)

    def forward(column):
        spec = outer_dot(outer[0], outer[1], column)
        real, imag = turn(spec[: 2 * LANES], spec[2 * LANES :], twid[0], -twid[1])
        spec = inner_dot(jnp.concatenate([real, imag], axis=1), inner[0], inner[1])
        return spec[:, :LANES], spec[:, LANES:]

    def inverse(real, imag):
        spec = inner_dot(jnp.concatenate([real, imag], axis=1), inner[2], inner[3])
        real, imag = turn(spec[:, :LANES], spec[:, LANES:], twid[0], twid[1])
        return outer_dot(last[0], last[1], jnp.concatenate([real, imag], axis=0))

    mine = filt_col.at[pl.ds(pl.multiple_of((seq ^ (trow & 3)) * quarter, quarter), quarter)]
    take(mine, recv_sem.at[0])
    for k in range(1, 4):
        pltpu.make_async_remote_copy(
            mine, mine, send_sem.at[3], recv_sem.at[3],
            device_id=(seq ^ k, trow, tcol), device_id_type=MESH,
        ).start()

    for load in loads[4:]:
        load.wait()
    take(value_col, recv_sem.at[1])
    value_real, value_imag = forward(value_col[...])
    take(filt_col.at[pl.ds(0, 3 * quarter)], recv_sem.at[3])
    filt_real, filt_imag = forward(filt_col[...])
    conv_col[...] = inverse(
        value_real * filt_real - value_imag * filt_imag,
        value_real * filt_imag + value_imag * filt_real,
    )
    to_rows(conv_col, conv_row, 4)

    take(grad_col, recv_sem.at[2])
    grad_real, grad_imag = forward(grad_col[...])
    corr = inverse(
        grad_real * value_real + grad_imag * value_imag,
        grad_imag * value_real - grad_real * value_imag,
    )
    corr_col[...] = corr
    for half in range(2):
        corr_parts[3 + half] = corr_col[pl.ds(half, LANES, stride=2), :]
    for half in range(2):
        owner = half * 2 + (me >> 6)

        @pl.when(owner != seq)
        def _():
            pltpu.make_async_remote_copy(
                corr_parts.at[3 + half], corr_parts.at[(seq ^ owner) - 1], send_sem.at[6 + half], recv_sem.at[6],
                device_id=(owner, trow, tcol), device_id_type=MESH,
            ).start()

    back_col[...] = inverse(
        grad_real * filt_real + grad_imag * filt_imag,
        grad_imag * filt_real - grad_real * filt_imag,
    )
    to_rows(back_col, back_row, 5)

    own_half = seq >> 1
    summing = (me >> 6) == (seq & 1)

    @pl.when(summing)
    def _():
        take(corr_parts.at[pl.ds(0, 3)], recv_sem.at[6])
        own = jnp.where(own_half == 0, corr_parts[3], corr_parts[4])
        corr_sum[...] = own + corr_parts[0] + corr_parts[1] + corr_parts[2]
        at = me & 63

        def send(peer_row, peer_col):
            pltpu.make_async_remote_copy(
                corr_sum.at[pl.ds(row_of(peer_row, peer_col), 1)], filt_out.at[pl.ds(at, 1)],
                send_sem.at[8], recv_sem.at[7],
                device_id=(seq, peer_row, peer_col), device_id_type=MESH,
            ).start()

        pltpu.make_async_copy(
            corr_sum.at[pl.ds(my_row, 1)], filt_out.at[pl.ds(at, 1)], recv_sem.at[7]
        ).start()
        each_peer(trow, tcol, send)

    def gather(rows):
        return jnp.concatenate(
            [rows[pl.ds(0, LANES, stride=2), :].T, rows[pl.ds(1, LANES, stride=2), :].T], axis=1
        )

    take(conv_row, recv_sem.at[4])
    gate_out[...] = (grad_in[...].astype(F32) * gather(conv_row)).astype(BF16)
    take(back_row, recv_sem.at[5])
    value_out[...] = gather(back_row).astype(BF16)
    take(filt_out, recv_sem.at[7])

    most = pl.ds(0, 2 * LANES - 2)

    @pl.when(seq == 0)
    def _():
        take(filt_send.at[pl.ds(0, quarter - 2)], send_sem.at[0])

    @pl.when(seq != 0)
    def _():
        take(filt_send.at[pl.ds(0, quarter)], send_sem.at[0])

    take(value_send.at[most], send_sem.at[1])
    take(grad_send.at[most], send_sem.at[2])
    take(filt_col.at[pl.ds(0, 3 * quarter)], send_sem.at[3])
    take(conv_col.at[most], send_sem.at[4])
    take(back_col.at[most], send_sem.at[5])
    for half in range(2):
        owner = half * 2 + (me >> 6)

        @pl.when(owner != seq)
        def _():
            take(corr_parts.at[3 + half], send_sem.at[6 + half])

    @pl.when(summing)
    def _():
        take(corr_sum.at[pl.ds(0, LANES - 1)], send_sem.at[8])


def store(gate_in, value_in, filt_in, gate_out, value_out, filt_out, sem):
    copies = [
        pltpu.make_async_copy(src, dst, sem.at[i])
        for i, (src, dst) in enumerate(((gate_in, gate_out), (value_in, value_out), (filt_in, filt_out)))
    ]
    for copy in copies:
        copy.start()
    for copy in copies:
        copy.wait()


def local(gate, value, grad_out, filter_raw):
    wide = pltpu.VMEM((2 * LANES, LANES), F32)
    bf16 = pltpu.VMEM((LANES, 2 * LANES), BF16)
    scratch = [
        bf16, bf16, bf16, pltpu.VMEM((LANES, 2 * LANES), F32),
        pltpu.VMEM((2, 4 * LANES, 2 * LANES), BF16),
        pltpu.VMEM((4, 2 * LANES, 2 * LANES), BF16),
        pltpu.VMEM((2, 2 * LANES, 4 * LANES), BF16),
        pltpu.VMEM((2, LANES, LANES), F32),
    ]
    scratch += [wide] * 11
    scratch += [
        pltpu.VMEM((5, LANES, LANES), F32),
        pltpu.VMEM((LANES, LANES), F32),
        pltpu.SemaphoreType.DMA((8,)),
        pltpu.SemaphoreType.DMA((9,)),
        pltpu.SemaphoreType.DMA((8,)),
    ]
    shapes = (
        jax.ShapeDtypeStruct((LANES, 2 * LANES), BF16),
        jax.ShapeDtypeStruct((LANES, 2 * LANES), BF16),
        jax.ShapeDtypeStruct((LANES // 2, LANES), F32),
    )
    results = pl.pallas_call(
        kernel,
        name="gated_conv_backward",
        out_shape=shapes,
        in_specs=[pl.BlockSpec(memory_space=pltpu.HBM)] * 8,
        out_specs=(pl.BlockSpec(memory_space=pltpu.VMEM),) * 3,
        scratch_shapes=scratch,
        compiler_params=pltpu.CompilerParams(
            collective_id=0, has_side_effects=True, vmem_limit_bytes=32 << 20
        ),
    )(*(pltpu.with_memory_space_constraint(x, pltpu.HBM) for x in (value[0], gate[0], grad_out[0], filter_raw, *(jnp.asarray(c) for c in constants()))))
    grad_gate, grad_value, grad_filter = pl.pallas_call(
        store,
        name="store_results",
        out_shape=shapes,
        in_specs=[pl.BlockSpec(memory_space=pltpu.VMEM)] * 3,
        out_specs=(pl.BlockSpec(memory_space=pltpu.HBM),) * 3,
        scratch_shapes=[pltpu.SemaphoreType.DMA((3,))],
    )(*(pltpu.with_memory_space_constraint(r, pltpu.VMEM) for r in results))
    return grad_gate[None], grad_value[None], grad_filter.T


def solution(mesh):
    tokens = P("dp", ("trow", "tcol"), None)
    return jax.shard_map(
        local,
        mesh=mesh,
        in_specs=(tokens, tokens, tokens, P(("trow", "tcol"), None)),
        out_specs=(tokens, tokens, P(("trow", "tcol"), "dp")),
        check_vma=False,
    )
```

```python
import functools

import jax
import jax.numpy as jnp
import ml_dtypes
import numpy as np
from jax import lax
from jax.experimental import pallas as pl
from jax.experimental.pallas import tpu as pltpu
from jax.sharding import PartitionSpec as P

MESH = pl.DeviceIdType.MESH
LANES = 128
F32 = jnp.float32
BF16 = jnp.bfloat16


def row_of(trow, tcol):
    return ((trow & 7) << 4) | ((trow >> 3) << 3) | tcol


def split_const(matrix):
    high = matrix.astype(np.float32).astype(ml_dtypes.bfloat16)
    low = (matrix - high.astype(np.float64)).astype(np.float32).astype(ml_dtypes.bfloat16)
    return high, low


def constants():
    block = np.zeros(LANES, np.int64)
    for trow in range(16):
        for tcol in range(8):
            block[row_of(trow, tcol)] = trow * 8 + tcol
    odd = 2 * np.arange(LANES) + 1
    theta = 2 * np.pi * ((odd[:, None] * block[None, :]) % 512) / 512
    wide = np.zeros((2, 2, LANES, LANES, 2))
    for half in range(2):
        wide[0, half, :, :, half] = np.cos(theta)
        wide[1, half, :, :, half] = -np.sin(theta)
    outer = wide.reshape(4 * LANES, 2 * LANES)
    place = np.arange(LANES)
    angle = 2 * np.pi * ((place[:, None] * place[None, :]) % LANES) / LANES
    cos, sin = np.cos(angle), np.sin(angle)
    inner = np.block([[cos, -sin], [sin, cos]])
    back = np.block([[cos, sin], [-sin, cos]])
    phi = 2 * np.pi * (odd[:, None] * place[None, :]) / 65536
    scale = 2.0 ** -21
    return (
        np.stack(split_const(outer)),
        np.stack(split_const(inner) + split_const(back)),
        np.stack(split_const(outer.T * scale)),
        np.stack([np.cos(phi), np.sin(phi)]).astype(np.float32),
    )


def peers_at(trow, tcol, dz, act, skip_me=False):
    y, z, core = (tcol & 6) | (trow >> 3), trow & 7, tcol & 1
    for dy in (4, 3, 5, 2, 6, 1, 7, 0):
        peer_y = (y + dy) & 7
        peer_row, peer_col = ((peer_y & 1) << 3) | ((z + dz) & 7), (peer_y & 6) | core
        act(peer_row, peer_col ^ 1)
        if dy or not skip_me:
            act(peer_row, peer_col)


def far_z(t):
    away = (t + 1) >> 1
    return jnp.where((t & 1) == 1, 4 - away, 4 + away)


def each_peer(trow, tcol, act):
    def step(t, carry):
        peers_at(trow, tcol, far_z(t), act)
        return carry

    lax.fori_loop(0, 7, step, 0)
    peers_at(trow, tcol, 0, act, True)


CUT = 2


def each_of_z(trow, tcol, part, act):
    y, z, core = (tcol & 6) | (trow >> 3), trow & 7, tcol & 1

    def step(peer_z, carry):
        for dy in (4, 3, 5, 2, 6, 1, 7, 0):
            peer_y = (y + dy) & 7
            peer_row, peer_col = ((peer_y & 1) << 3) | peer_z, (peer_y & 6) | core
            act(peer_row, peer_col ^ 1)
            if dy:
                act(peer_row, peer_col)
            else:
                pl.when(peer_z != z)(functools.partial(act, peer_row, peer_col))
        return carry

    lax.fori_loop((0, CUT)[part], (CUT, 8)[part], step, 0)


def halves(x):
    high = x.astype(BF16)
    low = (x - high.astype(F32)).astype(BF16)
    return high, low


def dot(a, b):
    return jnp.dot(a, b, preferred_element_type=F32)


def outer_dot(mat_high, mat_low, x):
    high, low = halves(x)
    both = dot(mat_high, jnp.concatenate([high, low], axis=1))
    return both[:, :LANES] + both[:, LANES:] + dot(mat_low, high)


def inner_dot(x, mat_high, mat_low):
    high, low = halves(x)
    return dot(high, mat_high) + dot(low, mat_high) + dot(high, mat_low)


def turn(real, imag, cos, sin):
    shape = (2, LANES, LANES)
    real, imag = real.reshape(shape), imag.reshape(shape)
    out_real = real * cos - imag * sin
    out_imag = imag * cos + real * sin
    return out_real.reshape(2 * LANES, LANES), out_imag.reshape(2 * LANES, LANES)


def kernel(
    value_hbm, gate_hbm, grad_hbm, filt_hbm, outer_hbm, inner_hbm, last_hbm, twid_hbm,
    gate_out, value_out, filt_out,
    value_in, gate_in, grad_in, filt_in, outer, inner, last, twid,
    value_send, filt_send,
    grad_send, value_col, grad_col, filt_col,
    conv_col, back_col, corr_col, conv_row, back_row,
    corr_parts, corr_sum, load_sem, send_sem, recv_sem, filt_sem,
):
    seq = lax.axis_index("dp")
    trow = lax.axis_index("trow")
    tcol = lax.axis_index("tcol")
    me = trow * 8 + tcol
    my_row = row_of(trow, tcol)

    barrier = pltpu.get_barrier_semaphore()

    def greet(peer_row, peer_col):
        pl.semaphore_signal(
            barrier, inc=1, device_id=(seq, peer_row, peer_col), device_id_type=MESH
        )

    each_peer(trow, tcol, greet)
    for k in range(1, 4):
        pl.semaphore_signal(
            barrier, inc=1, device_id=(seq ^ k, trow, tcol), device_id_type=MESH
        )

    loads = [
        pltpu.make_async_copy(src, dst, load_sem.at[i])
        for i, (src, dst) in enumerate(
            (
                (filt_hbm, filt_in),
                (value_hbm, value_in),
                (grad_hbm, grad_in),
                (gate_hbm, gate_in),
                (outer_hbm, outer),
                (inner_hbm, inner),
                (twid_hbm, twid),
                (last_hbm, last),
            )
        )
    ]
    for load in loads:
        load.start()

    def spread(rows, out):
        turned = rows.T
        for q in range(4):
            half, core = q // 2, 1 - q % 2
            out[pl.ds(2 * core + half, LANES // 2, stride=4), :] = turned[64 * q : 64 * q + 64]

    loads[0].wait()
    spread(filt_in[...], filt_send)
    loads[1].wait()
    spread(value_in[...].astype(F32), value_send)
    loads[2].wait()
    loads[3].wait()
    spread(grad_in[...].astype(F32) * gate_in[...].astype(F32), grad_send)

    pl.semaphore_wait(barrier, LANES - 1 + 3)

    def pair(ref, row):
        return ref.at[pl.ds(pl.multiple_of(row * 2, 2), 2)]

    def to_columns(src, dst, at):
        there = pair(dst, my_row)

        def send(peer_row, peer_col):
            pltpu.make_async_remote_copy(
                pair(src, peer_row * 8 + peer_col), there, send_sem.at[at], recv_sem.at[at],
                device_id=(seq, peer_row, peer_col), device_id_type=MESH,
            ).start()

        pltpu.make_async_copy(pair(src, me), there, recv_sem.at[at]).start()
        each_peer(trow, tcol, send)

    def to_rows(src, dst, at, part):
        there = pair(dst, me)

        def send(peer_row, peer_col):
            pltpu.make_async_remote_copy(
                pair(src, row_of(peer_row, peer_col)), there, send_sem.at[at], recv_sem.at[at],
                device_id=(seq, peer_row, peer_col), device_id_type=MESH,
            ).start()

        if part:
            pltpu.make_async_copy(pair(src, my_row), there, recv_sem.at[at]).start()
        each_of_z(trow, tcol, part, send)

    def take(view, sem):
        pltpu.make_async_copy(view, view, sem).wait()

    quarter = 2 * LANES // 4

    filt_there = pair(filt_col, my_row)

    def send_filt(peer_row, peer_col):
        pltpu.make_async_remote_copy(
            pair(filt_send, peer_row * 8 + peer_col), filt_there, send_sem.at[0], filt_sem.at[trow >> 2 & 1],
            device_id=(seq, peer_row, peer_col), device_id_type=MESH,
        ).start()

    for high in (4, 0):
        peer_z = ((trow ^ seq) & 3) | high
        for y_lo in (8, 0):
            for j in range(7, -1, -1):
                peer_row, peer_col = ((trow & 8) ^ y_lo) | peer_z, tcol ^ j
                if y_lo or j:
                    send_filt(peer_row, peer_col)
                else:
                    pl.when(peer_row != trow)(functools.partial(send_filt, peer_row, peer_col))

    @pl.when(seq == 0)
    def _():
        pltpu.make_async_copy(pair(filt_send, me), filt_there, filt_sem.at[trow >> 2 & 1]).start()

    to_columns(value_send, value_col, 1)
    to_columns(grad_send, grad_col, 2)

    def forward(column):
        spec = outer_dot(outer[0], outer[1], column)
        real, imag = turn(spec[: 2 * LANES], spec[2 * LANES :], twid[0], -twid[1])
        spec = inner_dot(jnp.concatenate([real, imag], axis=1), inner[0], inner[1])
        return spec[:, :LANES], spec[:, LANES:]

    def inverse(real, imag):
        spec = inner_dot(jnp.concatenate([real, imag], axis=1), inner[2], inner[3])
        real, imag = turn(spec[:, :LANES], spec[:, LANES:], twid[0], twid[1])
        return outer_dot(last[0], last[1], jnp.concatenate([real, imag], axis=0))

    for flip in range(2):
        high = (trow >> 2 & 1) ^ flip
        take(filt_col.at[pl.ds(0, 32)], filt_sem.at[high])
        block = filt_col.at[pl.ds(pl.multiple_of((((trow ^ seq) & 3) | (high << 2)) * 32, 32), 32)]
        for k in (2, 1, 3):
            pltpu.make_async_remote_copy(
                block, block, send_sem.at[3], recv_sem.at[3],
                device_id=(seq ^ k, trow, tcol), device_id_type=MESH,
            ).start()

    for load in loads[4:]:
        load.wait()
    take(value_col, recv_sem.at[1])
    value_real, value_imag = forward(value_col[...])
    take(grad_col, recv_sem.at[2])
    grad_real, grad_imag = forward(grad_col[...])
    corr_col[...] = inverse(
        grad_real * value_real + grad_imag * value_imag,
        grad_imag * value_real - grad_real * value_imag,
    )
    core = tcol & 1
    for half in range(2):
        corr_parts[3 + half] = corr_col[pl.ds(half, LANES, stride=2), :]
    owners = [half * 2 + 1 - core for half in range(2)]
    blocks = (pl.ds(0, 16 * CUT), pl.ds(16 * CUT, LANES - 16 * CUT))
    for part, at in enumerate(blocks):
        for half, owner in enumerate(owners):

            @pl.when(owner != seq)
            def _():
                pltpu.make_async_remote_copy(
                    corr_parts.at[3 + half, at], corr_parts.at[(seq ^ owner) - 1, at],
                    send_sem.at[6 + half], recv_sem.at[6 + part],
                    device_id=(owner, trow, tcol), device_id_type=MESH,
                ).start()

    take(filt_col.at[pl.ds(0, 3 * quarter)], recv_sem.at[3])
    filt_real, filt_imag = forward(filt_col[...])
    conv_col[...] = inverse(
        value_real * filt_real - value_imag * filt_imag,
        value_real * filt_imag + value_imag * filt_real,
    )
    to_rows(conv_col, conv_row, 4, 0)
    back_col[...] = inverse(
        grad_real * filt_real + grad_imag * filt_imag,
        grad_imag * filt_real - grad_real * filt_imag,
    )
    to_rows(back_col, back_row, 5, 0)

    own = 3 + (seq >> 1)
    summing = core != (seq & 1)
    filt_row = filt_out.at[pl.ds(me >> 1, 1)]

    def send_sum(peer_row, peer_col):
        pltpu.make_async_remote_copy(
            corr_sum.at[pl.ds(row_of(peer_row, peer_col), 1)], filt_row, send_sem.at[8], recv_sem.at[8],
            device_id=(seq, peer_row, peer_col), device_id_type=MESH,
        ).start()

    def send_sums(part):
        at = blocks[part]
        take(corr_parts.at[pl.ds(0, 3), at], recv_sem.at[6 + part])
        corr_sum[at] = corr_parts[own, at] + corr_parts[0, at] + corr_parts[1, at] + corr_parts[2, at]
        each_of_z(trow, tcol, part, send_sum)

    @pl.when(summing)
    def _():
        send_sums(0)

    to_rows(conv_col, conv_row, 4, 1)
    to_rows(back_col, back_row, 5, 1)

    @pl.when(summing)
    def _():
        send_sums(1)
        pltpu.make_async_copy(corr_sum.at[pl.ds(my_row, 1)], filt_row, recv_sem.at[8]).start()

    def gather(rows):
        return jnp.concatenate(
            [rows[pl.ds(2 * (1 - q % 2) + q // 2, LANES // 2, stride=4), :] for q in range(4)], axis=0
        ).T

    take(conv_row, recv_sem.at[4])
    gate_out[...] = (grad_in[...].astype(F32) * gather(conv_row)).astype(BF16)
    take(back_row, recv_sem.at[5])
    value_out[...] = gather(back_row).astype(BF16)
    take(filt_out, recv_sem.at[8])

    most = pl.ds(0, 2 * LANES - 2)

    @pl.when(seq == 0)
    def _():
        take(filt_send.at[pl.ds(0, quarter - 2)], send_sem.at[0])

    @pl.when(seq != 0)
    def _():
        take(filt_send.at[pl.ds(0, quarter)], send_sem.at[0])

    take(value_send.at[most], send_sem.at[1])
    take(grad_send.at[most], send_sem.at[2])
    take(filt_col.at[pl.ds(0, 3 * quarter)], send_sem.at[3])
    take(conv_col.at[most], send_sem.at[4])
    take(back_col.at[most], send_sem.at[5])
    for half, owner in enumerate(owners):

        @pl.when(owner != seq)
        def _():
            take(corr_parts.at[3 + half], send_sem.at[6 + half])

    @pl.when(summing)
    def _():
        take(corr_sum.at[pl.ds(0, LANES - 1)], send_sem.at[8])


def store(gate_in, value_in, filt_in, gate_out, value_out, filt_out, sem):
    copies = [
        pltpu.make_async_copy(src, dst, sem.at[i])
        for i, (src, dst) in enumerate(((gate_in, gate_out), (value_in, value_out), (filt_in, filt_out)))
    ]
    for copy in copies:
        copy.start()
    for copy in copies:
        copy.wait()


def local(gate, value, grad_out, filter_raw):
    wide = pltpu.VMEM((2 * LANES, LANES), F32)
    bf16 = pltpu.VMEM((LANES, 2 * LANES), BF16)
    scratch = [
        bf16, bf16, bf16, pltpu.VMEM((LANES, 2 * LANES), F32),
        pltpu.VMEM((2, 4 * LANES, 2 * LANES), BF16),
        pltpu.VMEM((4, 2 * LANES, 2 * LANES), BF16),
        pltpu.VMEM((2, 2 * LANES, 4 * LANES), BF16),
        pltpu.VMEM((2, LANES, LANES), F32),
    ]
    scratch += [wide] * 11
    scratch += [
        pltpu.VMEM((5, LANES, LANES), F32),
        pltpu.VMEM((LANES, LANES), F32),
        pltpu.SemaphoreType.DMA((8,)),
        pltpu.SemaphoreType.DMA((9,)),
        pltpu.SemaphoreType.DMA((9,)),
        pltpu.SemaphoreType.DMA((2,)),
    ]
    shapes = (
        jax.ShapeDtypeStruct((LANES, 2 * LANES), BF16),
        jax.ShapeDtypeStruct((LANES, 2 * LANES), BF16),
        jax.ShapeDtypeStruct((LANES // 2, LANES), F32),
    )
    results = pl.pallas_call(
        kernel,
        name="gated_conv_backward",
        out_shape=shapes,
        in_specs=[pl.BlockSpec(memory_space=pltpu.HBM)] * 8,
        out_specs=(pl.BlockSpec(memory_space=pltpu.VMEM),) * 3,
        scratch_shapes=scratch,
        compiler_params=pltpu.CompilerParams(
            collective_id=0, has_side_effects=True, vmem_limit_bytes=32 << 20
        ),
    )(*(pltpu.with_memory_space_constraint(x, pltpu.HBM) for x in (value[0], gate[0], grad_out[0], filter_raw, *(jnp.asarray(c) for c in constants()))))
    grad_gate, grad_value, grad_filter = pl.pallas_call(
        store,
        name="store_results",
        out_shape=shapes,
        in_specs=[pl.BlockSpec(memory_space=pltpu.VMEM)] * 3,
        out_specs=(pl.BlockSpec(memory_space=pltpu.HBM),) * 3,
        scratch_shapes=[pltpu.SemaphoreType.DMA((3,))],
    )(*(pltpu.with_memory_space_constraint(r, pltpu.VMEM) for r in results))
    return grad_gate[None], grad_value[None], grad_filter.T


def solution(mesh):
    tokens = P("dp", ("trow", "tcol"), None)
    return jax.shard_map(
        local,
        mesh=mesh,
        in_specs=(tokens, tokens, tokens, P(("trow", "tcol"), None)),
        out_specs=(tokens, tokens, P(("trow", "tcol"), "dp")),
        check_vma=False,
    )
```

```python
import functools

import jax
import jax.numpy as jnp
import ml_dtypes
import numpy as np
from jax import lax
from jax.experimental import pallas as pl
from jax.experimental.pallas import tpu as pltpu
from jax.sharding import PartitionSpec as P

MESH = pl.DeviceIdType.MESH
LANES = 128
F32 = jnp.float32
BF16 = jnp.bfloat16


def row_of(trow, tcol):
    return ((trow & 7) << 4) | ((trow >> 3) << 3) | tcol


def split_const(matrix):
    high = matrix.astype(np.float32).astype(ml_dtypes.bfloat16)
    low = (matrix - high.astype(np.float64)).astype(np.float32).astype(ml_dtypes.bfloat16)
    return high, low


def constants():
    block = np.zeros(LANES, np.int64)
    for trow in range(16):
        for tcol in range(8):
            block[row_of(trow, tcol)] = trow * 8 + tcol
    odd = 2 * np.arange(LANES) + 1
    theta = 2 * np.pi * ((odd[:, None] * block[None, :]) % 512) / 512
    wide = np.zeros((2, 2, LANES, 2, LANES))
    for half in range(2):
        wide[0, half, :, half] = np.cos(theta)
        wide[1, half, :, half] = -np.sin(theta)
    outer = wide.reshape(4 * LANES, 2 * LANES)
    place = np.arange(LANES)
    angle = 2 * np.pi * ((place[:, None] * place[None, :]) % LANES) / LANES
    cos, sin = np.cos(angle), np.sin(angle)
    inner = np.block([[cos, -sin], [sin, cos]])
    back = np.block([[cos, sin], [-sin, cos]])
    phi = 2 * np.pi * (odd[:, None] * place[None, :]) / 65536
    scale = 2.0 ** -21
    return (
        np.stack(split_const(outer)),
        np.stack(split_const(inner) + split_const(back)),
        np.stack(split_const(outer.T * scale)),
        np.stack([np.cos(phi), np.sin(phi)]).astype(np.float32),
    )


def peers_at(trow, tcol, dz, act, skip_me=False):
    y, z, core = (tcol & 6) | (trow >> 3), trow & 7, tcol & 1
    for dy in (4, 3, 5, 2, 6, 1, 7, 0):
        peer_y = (y + dy) & 7
        peer_row, peer_col = ((peer_y & 1) << 3) | ((z + dz) & 7), (peer_y & 6) | core
        act(peer_row, peer_col ^ 1)
        if dy or not skip_me:
            act(peer_row, peer_col)


def far_z(t):
    away = (t + 1) >> 1
    return jnp.where((t & 1) == 1, 4 - away, 4 + away)


def each_peer(trow, tcol, act):
    def step(t, carry):
        peers_at(trow, tcol, far_z(t), act)
        return carry

    lax.fori_loop(0, 7, step, 0)
    peers_at(trow, tcol, 0, act, True)


CUT = 2


def each_of_z(trow, tcol, part, act):
    y, z, core = (tcol & 6) | (trow >> 3), trow & 7, tcol & 1

    def step(peer_z, carry):
        for dy in (4, 3, 5, 2, 6, 1, 7, 0):
            peer_y = (y + dy) & 7
            peer_row, peer_col = ((peer_y & 1) << 3) | peer_z, (peer_y & 6) | core
            act(peer_row, peer_col ^ 1)
            if dy:
                act(peer_row, peer_col)
            else:
                pl.when(peer_z != z)(functools.partial(act, peer_row, peer_col))
        return carry

    lax.fori_loop((0, CUT)[part], (CUT, 8)[part], step, 0)


def halves(x):
    high = x.astype(BF16)
    low = (x - high.astype(F32)).astype(BF16)
    return high, low


def dot(a, b):
    return jnp.dot(a, b, preferred_element_type=F32)


def outer_dot(mat_high, mat_low, x):
    high, low = halves(x)
    both = dot(mat_high, jnp.concatenate([high, low], axis=1))
    return both[:, :LANES] + both[:, LANES:] + dot(mat_low, high)


def inner_dot(x, mat_high, mat_low):
    high, low = halves(x)
    return dot(high, mat_high) + dot(low, mat_high) + dot(high, mat_low)


def turn(real, imag, cos, sin):
    shape = (2, LANES, LANES)
    real, imag = real.reshape(shape), imag.reshape(shape)
    out_real = real * cos - imag * sin
    out_imag = imag * cos + real * sin
    return out_real.reshape(2 * LANES, LANES), out_imag.reshape(2 * LANES, LANES)


def kernel(
    value_hbm, gate_hbm, grad_hbm, filt_hbm, outer_hbm, inner_hbm, last_hbm, twid_hbm,
    gate_out, value_out, filt_out,
    value_in, gate_in, grad_in, filt_in, outer, inner, last, twid,
    both_send, filt_send, both_col, filt_col,
    conv_col, back_col, conv_row, back_row,
    corr_parts, corr_sum, load_sem, send_sem, recv_sem, filt_sem,
):
    seq = lax.axis_index("dp")
    trow = lax.axis_index("trow")
    tcol = lax.axis_index("tcol")
    me = trow * 8 + tcol
    my_row = row_of(trow, tcol)

    barrier = pltpu.get_barrier_semaphore()

    def greet(peer_row, peer_col):
        pl.semaphore_signal(
            barrier, inc=1, device_id=(seq, peer_row, peer_col), device_id_type=MESH
        )

    each_peer(trow, tcol, greet)
    for k in range(1, 4):
        pl.semaphore_signal(
            barrier, inc=1, device_id=(seq ^ k, trow, tcol), device_id_type=MESH
        )

    loads = [
        pltpu.make_async_copy(src, dst, load_sem.at[i])
        for i, (src, dst) in enumerate(
            (
                (filt_hbm, filt_in),
                (value_hbm, value_in),
                (grad_hbm, grad_in),
                (gate_hbm, gate_in),
                (outer_hbm, outer),
                (inner_hbm, inner),
                (twid_hbm, twid),
                (last_hbm, last),
            )
        )
    ]
    for load in loads:
        load.start()

    def spread(rows, out, first, count):
        turned = rows.T
        for q in range(4):
            half, core = q // 2, 1 - q % 2
            out[pl.ds(count * core + first + half, LANES // 2, stride=2 * count), :] = turned[64 * q : 64 * q + 64]

    loads[0].wait()
    spread(filt_in[...], filt_send, 0, 2)
    loads[1].wait()
    spread(value_in[...].astype(F32), both_send, 0, 4)
    loads[2].wait()
    loads[3].wait()
    spread(grad_in[...].astype(F32) * gate_in[...].astype(F32), both_send, 2, 4)

    pl.semaphore_wait(barrier, LANES - 1 + 3)

    def pair(ref, row):
        return ref.at[pl.ds(pl.multiple_of(row * 2, 2), 2)]

    def four(ref, row):
        return ref.at[pl.ds(pl.multiple_of(row * 4, 4), 4)]

    def by_channel(ref, first, count):
        return jnp.concatenate([ref[pl.ds(first + half, LANES, stride=count), :] for half in range(2)], axis=0)

    def to_columns(src, dst, at):
        there = four(dst, my_row)

        def send(peer_row, peer_col):
            pltpu.make_async_remote_copy(
                four(src, peer_row * 8 + peer_col), there, send_sem.at[at], recv_sem.at[at],
                device_id=(seq, peer_row, peer_col), device_id_type=MESH,
            ).start()

        pltpu.make_async_copy(four(src, me), there, recv_sem.at[at]).start()
        each_peer(trow, tcol, send)

    def to_rows(src, dst, at, part):
        there = pair(dst, me)

        def send(peer_row, peer_col):
            pltpu.make_async_remote_copy(
                pair(src, row_of(peer_row, peer_col)), there, send_sem.at[at], recv_sem.at[at],
                device_id=(seq, peer_row, peer_col), device_id_type=MESH,
            ).start()

        if part:
            pltpu.make_async_copy(pair(src, my_row), there, recv_sem.at[at]).start()
        each_of_z(trow, tcol, part, send)

    def take(view, sem):
        pltpu.make_async_copy(view, view, sem).wait()

    quarter = 2 * LANES // 4

    filt_there = pair(filt_col, my_row)

    def send_filt(peer_row, peer_col):
        pltpu.make_async_remote_copy(
            pair(filt_send, peer_row * 8 + peer_col), filt_there, send_sem.at[0], filt_sem.at[trow >> 2 & 1],
            device_id=(seq, peer_row, peer_col), device_id_type=MESH,
        ).start()

    for high in (4, 0):
        peer_z = ((trow ^ seq) & 3) | high
        for y_lo in (8, 0):
            for j in range(7, -1, -1):
                peer_row, peer_col = ((trow & 8) ^ y_lo) | peer_z, tcol ^ j
                if y_lo or j:
                    send_filt(peer_row, peer_col)
                else:
                    pl.when(peer_row != trow)(functools.partial(send_filt, peer_row, peer_col))

    @pl.when(seq == 0)
    def _():
        pltpu.make_async_copy(pair(filt_send, me), filt_there, filt_sem.at[trow >> 2 & 1]).start()

    to_columns(both_send, both_col, 1)

    def forward(column):
        spec = outer_dot(outer[0], outer[1], column)
        real, imag = turn(spec[: 2 * LANES], spec[2 * LANES :], twid[0], -twid[1])
        spec = inner_dot(jnp.concatenate([real, imag], axis=1), inner[0], inner[1])
        return spec[:, :LANES], spec[:, LANES:]

    def inverse(real, imag):
        spec = inner_dot(jnp.concatenate([real, imag], axis=1), inner[2], inner[3])
        real, imag = turn(spec[:, :LANES], spec[:, LANES:], twid[0], twid[1])
        return outer_dot(last[0], last[1], jnp.concatenate([real, imag], axis=0))

    for flip in range(2):
        high = (trow >> 2 & 1) ^ flip
        take(filt_col.at[pl.ds(0, 32)], filt_sem.at[high])
        block = filt_col.at[pl.ds(pl.multiple_of((((trow ^ seq) & 3) | (high << 2)) * 32, 32), 32)]
        for k in (2, 1, 3):
            pltpu.make_async_remote_copy(
                block, block, send_sem.at[3], recv_sem.at[3],
                device_id=(seq ^ k, trow, tcol), device_id_type=MESH,
            ).start()

    for load in loads[4:]:
        load.wait()
    take(both_col, recv_sem.at[1])
    value_real, value_imag = forward(by_channel(both_col, 0, 4))
    grad_real, grad_imag = forward(by_channel(both_col, 2, 4))
    corr = inverse(
        grad_real * value_real + grad_imag * value_imag,
        grad_imag * value_real - grad_real * value_imag,
    )
    core = tcol & 1
    for half in range(2):
        corr_parts[3 + half] = corr[half * LANES : half * LANES + LANES]
    owners = [half * 2 + 1 - core for half in range(2)]
    blocks = (pl.ds(0, 16 * CUT), pl.ds(16 * CUT, LANES - 16 * CUT))
    for part, at in enumerate(blocks):
        for half, owner in enumerate(owners):

            @pl.when(owner != seq)
            def _():
                pltpu.make_async_remote_copy(
                    corr_parts.at[3 + half, at], corr_parts.at[(seq ^ owner) - 1, at],
                    send_sem.at[6 + half], recv_sem.at[6 + part],
                    device_id=(owner, trow, tcol), device_id_type=MESH,
                ).start()

    take(filt_col.at[pl.ds(0, 3 * quarter)], recv_sem.at[3])
    filt_real, filt_imag = forward(by_channel(filt_col, 0, 2))
    def put(ref, result):
        for half in range(2):
            ref[pl.ds(half, LANES, stride=2), :] = result[half * LANES : half * LANES + LANES]

    conv = inverse(
        value_real * filt_real - value_imag * filt_imag,
        value_real * filt_imag + value_imag * filt_real,
    )
    put(conv_col, conv)
    to_rows(conv_col, conv_row, 4, 0)
    back = inverse(
        grad_real * filt_real + grad_imag * filt_imag,
        grad_imag * filt_real - grad_real * filt_imag,
    )
    put(back_col, back)
    to_rows(back_col, back_row, 5, 0)

    own = 3 + (seq >> 1)
    summing = core != (seq & 1)
    filt_row = filt_out.at[pl.ds(me >> 1, 1)]

    def send_sum(peer_row, peer_col):
        pltpu.make_async_remote_copy(
            corr_sum.at[pl.ds(row_of(peer_row, peer_col), 1)], filt_row, send_sem.at[8], recv_sem.at[8],
            device_id=(seq, peer_row, peer_col), device_id_type=MESH,
        ).start()

    def send_sums(part):
        at = blocks[part]
        take(corr_parts.at[pl.ds(0, 3), at], recv_sem.at[6 + part])
        corr_sum[at] = corr_parts[own, at] + corr_parts[0, at] + corr_parts[1, at] + corr_parts[2, at]
        each_of_z(trow, tcol, part, send_sum)

    @pl.when(summing)
    def _():
        send_sums(0)

    to_rows(conv_col, conv_row, 4, 1)
    to_rows(back_col, back_row, 5, 1)

    @pl.when(summing)
    def _():
        send_sums(1)
        pltpu.make_async_copy(corr_sum.at[pl.ds(my_row, 1)], filt_row, recv_sem.at[8]).start()

    def gather(rows):
        return jnp.concatenate(
            [rows[pl.ds(2 * (1 - q % 2) + q // 2, LANES // 2, stride=4), :] for q in range(4)], axis=0
        ).T

    take(conv_row, recv_sem.at[4])
    gate_out[...] = (grad_in[...].astype(F32) * gather(conv_row)).astype(BF16)
    take(back_row, recv_sem.at[5])
    value_out[...] = gather(back_row).astype(BF16)
    take(filt_out, recv_sem.at[8])

    most = pl.ds(0, 2 * LANES - 2)

    @pl.when(seq == 0)
    def _():
        take(filt_send.at[pl.ds(0, quarter - 2)], send_sem.at[0])

    @pl.when(seq != 0)
    def _():
        take(filt_send.at[pl.ds(0, quarter)], send_sem.at[0])

    take(both_send.at[pl.ds(0, 4 * LANES - 4)], send_sem.at[1])
    take(filt_col.at[pl.ds(0, 3 * quarter)], send_sem.at[3])
    take(conv_col.at[most], send_sem.at[4])
    take(back_col.at[most], send_sem.at[5])
    for half, owner in enumerate(owners):

        @pl.when(owner != seq)
        def _():
            take(corr_parts.at[3 + half], send_sem.at[6 + half])

    @pl.when(summing)
    def _():
        take(corr_sum.at[pl.ds(0, LANES - 1)], send_sem.at[8])


def store(gate_in, value_in, filt_in, gate_out, value_out, filt_out, sem):
    copies = [
        pltpu.make_async_copy(src, dst, sem.at[i])
        for i, (src, dst) in enumerate(((gate_in, gate_out), (value_in, value_out), (filt_in, filt_out)))
    ]
    for copy in copies:
        copy.start()
    for copy in copies:
        copy.wait()


def local(gate, value, grad_out, filter_raw):
    wide = pltpu.VMEM((2 * LANES, LANES), F32)
    bf16 = pltpu.VMEM((LANES, 2 * LANES), BF16)
    scratch = [
        bf16, bf16, bf16, pltpu.VMEM((LANES, 2 * LANES), F32),
        pltpu.VMEM((2, 4 * LANES, 2 * LANES), BF16),
        pltpu.VMEM((4, 2 * LANES, 2 * LANES), BF16),
        pltpu.VMEM((2, 2 * LANES, 4 * LANES), BF16),
        pltpu.VMEM((2, LANES, LANES), F32),
    ]
    double = pltpu.VMEM((4 * LANES, LANES), F32)
    scratch += [double, wide, double, wide] + [wide] * 4
    scratch += [
        pltpu.VMEM((5, LANES, LANES), F32),
        pltpu.VMEM((LANES, LANES), F32),
        pltpu.SemaphoreType.DMA((8,)),
        pltpu.SemaphoreType.DMA((9,)),
        pltpu.SemaphoreType.DMA((9,)),
        pltpu.SemaphoreType.DMA((2,)),
    ]
    shapes = (
        jax.ShapeDtypeStruct((LANES, 2 * LANES), BF16),
        jax.ShapeDtypeStruct((LANES, 2 * LANES), BF16),
        jax.ShapeDtypeStruct((LANES // 2, LANES), F32),
    )
    results = pl.pallas_call(
        kernel,
        name="gated_conv_backward",
        out_shape=shapes,
        in_specs=[pl.BlockSpec(memory_space=pltpu.HBM)] * 8,
        out_specs=(pl.BlockSpec(memory_space=pltpu.VMEM),) * 3,
        scratch_shapes=scratch,
        compiler_params=pltpu.CompilerParams(
            collective_id=0, has_side_effects=True, vmem_limit_bytes=32 << 20
        ),
    )(*(pltpu.with_memory_space_constraint(x, pltpu.HBM) for x in (value[0], gate[0], grad_out[0], filter_raw, *(jnp.asarray(c) for c in constants()))))
    grad_gate, grad_value, grad_filter = pl.pallas_call(
        store,
        name="store_results",
        out_shape=shapes,
        in_specs=[pl.BlockSpec(memory_space=pltpu.VMEM)] * 3,
        out_specs=(pl.BlockSpec(memory_space=pltpu.HBM),) * 3,
        scratch_shapes=[pltpu.SemaphoreType.DMA((3,))],
    )(*(pltpu.with_memory_space_constraint(r, pltpu.VMEM) for r in results))
    return grad_gate[None], grad_value[None], grad_filter.T


def solution(mesh):
    tokens = P("dp", ("trow", "tcol"), None)
    return jax.shard_map(
        local,
        mesh=mesh,
        in_specs=(tokens, tokens, tokens, P(("trow", "tcol"), None)),
        out_specs=(tokens, tokens, P(("trow", "tcol"), "dp")),
        check_vma=False,
    )
```

```python
import functools

import jax
import jax.numpy as jnp
import ml_dtypes
import numpy as np
from jax import lax
from jax.experimental import pallas as pl
from jax.experimental.pallas import tpu as pltpu
from jax.sharding import PartitionSpec as P

MESH = pl.DeviceIdType.MESH
LANES = 128
F32 = jnp.float32
BF16 = jnp.bfloat16


def row_of(trow, tcol):
    return ((trow & 7) << 4) | ((trow >> 3) << 3) | tcol


def split_const(matrix):
    high = matrix.astype(np.float32).astype(ml_dtypes.bfloat16)
    low = (matrix - high.astype(np.float64)).astype(np.float32).astype(ml_dtypes.bfloat16)
    return high, low


def constants():
    block = np.zeros(LANES, np.int64)
    for trow in range(16):
        for tcol in range(8):
            block[row_of(trow, tcol)] = trow * 8 + tcol
    odd = 2 * np.arange(LANES) + 1
    theta = 2 * np.pi * ((odd[:, None] * block[None, :]) % 512) / 512
    wide = np.zeros((2, 2, LANES, 2, LANES))
    for half in range(2):
        wide[0, half, :, half] = np.cos(theta)
        wide[1, half, :, half] = -np.sin(theta)
    outer = wide.reshape(4 * LANES, 2 * LANES)
    place = np.arange(LANES)
    angle = 2 * np.pi * ((place[:, None] * place[None, :]) % LANES) / LANES
    cos, sin = np.cos(angle), np.sin(angle)
    inner = np.block([[cos, -sin], [sin, cos]])
    back = np.block([[cos, sin], [-sin, cos]])
    phi = 2 * np.pi * (odd[:, None] * place[None, :]) / 65536
    scale = 2.0 ** -21
    return (
        np.stack(split_const(outer)),
        np.stack(split_const(inner) + split_const(back)),
        np.stack(split_const(outer.T * scale)),
        np.stack([np.cos(phi), np.sin(phi)]).astype(np.float32),
    )


def peers_at(trow, tcol, dz, act, skip_me=False):
    y, z, core = (tcol & 6) | (trow >> 3), trow & 7, tcol & 1
    for dy in (4, 3, 5, 2, 6, 1, 7, 0):
        peer_y = (y + dy) & 7
        peer_row, peer_col = ((peer_y & 1) << 3) | ((z + dz) & 7), (peer_y & 6) | core
        act(peer_row, peer_col ^ 1)
        if dy or not skip_me:
            act(peer_row, peer_col)


def far_z(t):
    away = (t + 1) >> 1
    return jnp.where((t & 1) == 1, 4 - away, 4 + away)


def each_peer(trow, tcol, act):
    def step(t, carry):
        peers_at(trow, tcol, far_z(t), act)
        return carry

    lax.fori_loop(0, 7, step, 0)
    peers_at(trow, tcol, 0, act, True)


CUT = 2


def each_of_z(trow, tcol, part, act):
    y, z, core = (tcol & 6) | (trow >> 3), trow & 7, tcol & 1

    def step(peer_z, carry):
        for peer_y in range(8):
            peer_row, peer_col = ((peer_y & 1) << 3) | peer_z, (peer_y & 6) | core
            act(peer_row, peer_col ^ 1)
            pl.when((peer_z != z) | (y != peer_y))(functools.partial(act, peer_row, peer_col))
        return carry

    lax.fori_loop((0, CUT)[part], (CUT, 8)[part], step, 0)


def halves(x):
    high = x.astype(BF16)
    low = (x - high.astype(F32)).astype(BF16)
    return high, low


def dot(a, b):
    return jnp.dot(a, b, preferred_element_type=F32)


def outer_dot(mat_high, mat_low, x):
    high, low = halves(x)
    both = dot(mat_high, jnp.concatenate([high, low], axis=1))
    return both[:, :LANES] + both[:, LANES:] + dot(mat_low, high)


def inner_dot(x, mat_high, mat_low):
    high, low = halves(x)
    return dot(high, mat_high) + dot(low, mat_high) + dot(high, mat_low)


def turn(real, imag, cos, sin):
    shape = (2, LANES, LANES)
    real, imag = real.reshape(shape), imag.reshape(shape)
    out_real = real * cos - imag * sin
    out_imag = imag * cos + real * sin
    return out_real.reshape(2 * LANES, LANES), out_imag.reshape(2 * LANES, LANES)


def kernel(
    value_hbm, gate_hbm, grad_hbm, filt_hbm, outer_hbm, inner_hbm, last_hbm, twid_hbm,
    gate_out, value_out, filt_out,
    value_in, gate_in, grad_in, filt_in, outer, inner, last, twid,
    both_send, filt_send, both_col, filt_col,
    conv_col, back_col, conv_row, back_row,
    corr_parts, corr_sum, load_sem, send_sem, recv_sem, filt_sem,
):
    seq = lax.axis_index("dp")
    trow = lax.axis_index("trow")
    tcol = lax.axis_index("tcol")
    me = trow * 8 + tcol
    my_row = row_of(trow, tcol)

    barrier = pltpu.get_barrier_semaphore()

    def greet(peer_row, peer_col):
        pl.semaphore_signal(
            barrier, inc=1, device_id=(seq, peer_row, peer_col), device_id_type=MESH
        )

    each_peer(trow, tcol, greet)
    for k in range(1, 4):
        pl.semaphore_signal(
            barrier, inc=1, device_id=(seq ^ k, trow, tcol), device_id_type=MESH
        )

    loads = [
        pltpu.make_async_copy(src, dst, load_sem.at[i])
        for i, (src, dst) in enumerate(
            (
                (filt_hbm, filt_in),
                (value_hbm, value_in),
                (grad_hbm, grad_in),
                (gate_hbm, gate_in),
                (outer_hbm, outer),
                (inner_hbm, inner),
                (twid_hbm, twid),
                (last_hbm, last),
            )
        )
    ]
    for load in loads:
        load.start()

    def spread(rows, out, first, count):
        turned = rows.T
        for q in range(4):
            half, core = q // 2, 1 - q % 2
            out[pl.ds(count * core + first + half, LANES // 2, stride=2 * count), :] = turned[64 * q : 64 * q + 64]

    loads[0].wait()
    spread(filt_in[...], filt_send, 0, 2)
    loads[1].wait()
    spread(value_in[...].astype(F32), both_send, 0, 4)
    loads[2].wait()
    loads[3].wait()
    spread(grad_in[...].astype(F32) * gate_in[...].astype(F32), both_send, 2, 4)

    pl.semaphore_wait(barrier, LANES - 1 + 3)

    def pair(ref, row):
        return ref.at[pl.ds(pl.multiple_of(row * 2, 2), 2)]

    def four(ref, row):
        return ref.at[pl.ds(pl.multiple_of(row * 4, 4), 4)]

    def by_channel(ref, first, count):
        return jnp.concatenate([ref[pl.ds(first + half, LANES, stride=count), :] for half in range(2)], axis=0)

    def to_columns(src, dst, at):
        there = four(dst, my_row)

        def send(peer_row, peer_col):
            pltpu.make_async_remote_copy(
                four(src, peer_row * 8 + peer_col), there, send_sem.at[at], recv_sem.at[at],
                device_id=(seq, peer_row, peer_col), device_id_type=MESH,
            ).start()

        pltpu.make_async_copy(four(src, me), there, recv_sem.at[at]).start()
        each_peer(trow, tcol, send)

    def to_rows(src, dst, at, part):
        there = pair(dst, me)

        def send(peer_row, peer_col):
            pltpu.make_async_remote_copy(
                pair(src, row_of(peer_row, peer_col)), there, send_sem.at[at], recv_sem.at[at],
                device_id=(seq, peer_row, peer_col), device_id_type=MESH,
            ).start()

        if part:
            pltpu.make_async_copy(pair(src, my_row), there, recv_sem.at[at]).start()
        each_of_z(trow, tcol, part, send)

    def take(view, sem):
        pltpu.make_async_copy(view, view, sem).wait()

    quarter = 2 * LANES // 4

    filt_there = pair(filt_col, my_row)

    def send_filt(peer_row, peer_col):
        pltpu.make_async_remote_copy(
            pair(filt_send, peer_row * 8 + peer_col), filt_there, send_sem.at[0], filt_sem.at[trow >> 2 & 1],
            device_id=(seq, peer_row, peer_col), device_id_type=MESH,
        ).start()

    for high in (4, 0):
        peer_z = ((trow ^ seq) & 3) | high
        for y_lo in (8, 0):
            for j in range(7, -1, -1):
                peer_row, peer_col = ((trow & 8) ^ y_lo) | peer_z, tcol ^ j
                if y_lo or j:
                    send_filt(peer_row, peer_col)
                else:
                    pl.when(peer_row != trow)(functools.partial(send_filt, peer_row, peer_col))

    @pl.when(seq == 0)
    def _():
        pltpu.make_async_copy(pair(filt_send, me), filt_there, filt_sem.at[trow >> 2 & 1]).start()

    to_columns(both_send, both_col, 1)

    def forward(column):
        spec = outer_dot(outer[0], outer[1], column)
        real, imag = turn(spec[: 2 * LANES], spec[2 * LANES :], twid[0], -twid[1])
        spec = inner_dot(jnp.concatenate([real, imag], axis=1), inner[0], inner[1])
        return spec[:, :LANES], spec[:, LANES:]

    def inverse(real, imag):
        spec = inner_dot(jnp.concatenate([real, imag], axis=1), inner[2], inner[3])
        real, imag = turn(spec[:, :LANES], spec[:, LANES:], twid[0], twid[1])
        return outer_dot(last[0], last[1], jnp.concatenate([real, imag], axis=0))

    for flip in range(2):
        high = (trow >> 2 & 1) ^ flip
        take(filt_col.at[pl.ds(0, 32)], filt_sem.at[high])
        block = filt_col.at[pl.ds(pl.multiple_of((((trow ^ seq) & 3) | (high << 2)) * 32, 32), 32)]
        for k in (2, 1, 3):
            pltpu.make_async_remote_copy(
                block, block, send_sem.at[3], recv_sem.at[3],
                device_id=(seq ^ k, trow, tcol), device_id_type=MESH,
            ).start()

    for load in loads[4:]:
        load.wait()
    take(both_col, recv_sem.at[1])
    value_real, value_imag = forward(by_channel(both_col, 0, 4))
    grad_real, grad_imag = forward(by_channel(both_col, 2, 4))
    corr = inverse(
        grad_real * value_real + grad_imag * value_imag,
        grad_imag * value_real - grad_real * value_imag,
    )
    core = tcol & 1
    for half in range(2):
        corr_parts[3 + half] = corr[half * LANES : half * LANES + LANES]
    owners = [half * 2 + 1 - core for half in range(2)]
    blocks = (pl.ds(0, 16 * CUT), pl.ds(16 * CUT, LANES - 16 * CUT))
    for part, at in enumerate(blocks):
        for half, owner in enumerate(owners):

            @pl.when(owner != seq)
            def _():
                pltpu.make_async_remote_copy(
                    corr_parts.at[3 + half, at], corr_parts.at[(seq ^ owner) - 1, at],
                    send_sem.at[6 + half], recv_sem.at[6 + part],
                    device_id=(owner, trow, tcol), device_id_type=MESH,
                ).start()

    take(filt_col.at[pl.ds(0, 3 * quarter)], recv_sem.at[3])
    filt_real, filt_imag = forward(by_channel(filt_col, 0, 2))
    def put(ref, result):
        for half in range(2):
            ref[pl.ds(half, LANES, stride=2), :] = result[half * LANES : half * LANES + LANES]

    conv = inverse(
        value_real * filt_real - value_imag * filt_imag,
        value_real * filt_imag + value_imag * filt_real,
    )
    put(conv_col, conv)
    to_rows(conv_col, conv_row, 4, 0)
    back = inverse(
        grad_real * filt_real + grad_imag * filt_imag,
        grad_imag * filt_real - grad_real * filt_imag,
    )
    put(back_col, back)
    to_rows(back_col, back_row, 5, 0)

    own = 3 + (seq >> 1)
    summing = core != (seq & 1)
    filt_row = filt_out.at[pl.ds(me >> 1, 1)]

    def send_sum(peer_row, peer_col):
        pltpu.make_async_remote_copy(
            corr_sum.at[pl.ds(row_of(peer_row, peer_col), 1)], filt_row, send_sem.at[8], recv_sem.at[8],
            device_id=(seq, peer_row, peer_col), device_id_type=MESH,
        ).start()

    def send_sums(part):
        at = blocks[part]
        take(corr_parts.at[pl.ds(0, 3), at], recv_sem.at[6 + part])
        corr_sum[at] = corr_parts[own, at] + corr_parts[0, at] + corr_parts[1, at] + corr_parts[2, at]
        each_of_z(trow, tcol, part, send_sum)

    @pl.when(summing)
    def _():
        send_sums(0)

    to_rows(conv_col, conv_row, 4, 1)
    to_rows(back_col, back_row, 5, 1)

    @pl.when(summing)
    def _():
        send_sums(1)
        pltpu.make_async_copy(corr_sum.at[pl.ds(my_row, 1)], filt_row, recv_sem.at[8]).start()

    def gather(rows):
        return jnp.concatenate(
            [rows[pl.ds(2 * (1 - q % 2) + q // 2, LANES // 2, stride=4), :] for q in range(4)], axis=0
        ).T

    take(conv_row, recv_sem.at[4])
    gate_out[...] = (grad_in[...].astype(F32) * gather(conv_row)).astype(BF16)
    take(back_row, recv_sem.at[5])
    value_out[...] = gather(back_row).astype(BF16)
    take(filt_out, recv_sem.at[8])

    most = pl.ds(0, 2 * LANES - 2)

    @pl.when(seq == 0)
    def _():
        take(filt_send.at[pl.ds(0, quarter - 2)], send_sem.at[0])

    @pl.when(seq != 0)
    def _():
        take(filt_send.at[pl.ds(0, quarter)], send_sem.at[0])

    take(both_send.at[pl.ds(0, 4 * LANES - 4)], send_sem.at[1])
    take(filt_col.at[pl.ds(0, 3 * quarter)], send_sem.at[3])
    take(conv_col.at[most], send_sem.at[4])
    take(back_col.at[most], send_sem.at[5])
    for half, owner in enumerate(owners):

        @pl.when(owner != seq)
        def _():
            take(corr_parts.at[3 + half], send_sem.at[6 + half])

    @pl.when(summing)
    def _():
        take(corr_sum.at[pl.ds(0, LANES - 1)], send_sem.at[8])


def store(gate_in, value_in, filt_in, gate_out, value_out, filt_out, sem):
    copies = [
        pltpu.make_async_copy(src, dst, sem.at[i])
        for i, (src, dst) in enumerate(((gate_in, gate_out), (value_in, value_out), (filt_in, filt_out)))
    ]
    for copy in copies:
        copy.start()
    for copy in copies:
        copy.wait()


def local(gate, value, grad_out, filter_raw):
    wide = pltpu.VMEM((2 * LANES, LANES), F32)
    bf16 = pltpu.VMEM((LANES, 2 * LANES), BF16)
    scratch = [
        bf16, bf16, bf16, pltpu.VMEM((LANES, 2 * LANES), F32),
        pltpu.VMEM((2, 4 * LANES, 2 * LANES), BF16),
        pltpu.VMEM((4, 2 * LANES, 2 * LANES), BF16),
        pltpu.VMEM((2, 2 * LANES, 4 * LANES), BF16),
        pltpu.VMEM((2, LANES, LANES), F32),
    ]
    double = pltpu.VMEM((4 * LANES, LANES), F32)
    scratch += [double, wide, double, wide] + [wide] * 4
    scratch += [
        pltpu.VMEM((5, LANES, LANES), F32),
        pltpu.VMEM((LANES, LANES), F32),
        pltpu.SemaphoreType.DMA((8,)),
        pltpu.SemaphoreType.DMA((9,)),
        pltpu.SemaphoreType.DMA((9,)),
        pltpu.SemaphoreType.DMA((2,)),
    ]
    shapes = (
        jax.ShapeDtypeStruct((LANES, 2 * LANES), BF16),
        jax.ShapeDtypeStruct((LANES, 2 * LANES), BF16),
        jax.ShapeDtypeStruct((LANES // 2, LANES), F32),
    )
    results = pl.pallas_call(
        kernel,
        name="gated_conv_backward",
        out_shape=shapes,
        in_specs=[pl.BlockSpec(memory_space=pltpu.HBM)] * 8,
        out_specs=(pl.BlockSpec(memory_space=pltpu.VMEM),) * 3,
        scratch_shapes=scratch,
        compiler_params=pltpu.CompilerParams(
            collective_id=0, has_side_effects=True, vmem_limit_bytes=32 << 20
        ),
    )(*(pltpu.with_memory_space_constraint(x, pltpu.HBM) for x in (value[0], gate[0], grad_out[0], filter_raw, *(jnp.asarray(c) for c in constants()))))
    grad_gate, grad_value, grad_filter = pl.pallas_call(
        store,
        name="store_results",
        out_shape=shapes,
        in_specs=[pl.BlockSpec(memory_space=pltpu.VMEM)] * 3,
        out_specs=(pl.BlockSpec(memory_space=pltpu.HBM),) * 3,
        scratch_shapes=[pltpu.SemaphoreType.DMA((3,))],
    )(*(pltpu.with_memory_space_constraint(r, pltpu.VMEM) for r in results))
    return grad_gate[None], grad_value[None], grad_filter.T


def solution(mesh):
    tokens = P("dp", ("trow", "tcol"), None)
    return jax.shard_map(
        local,
        mesh=mesh,
        in_specs=(tokens, tokens, tokens, P(("trow", "tcol"), None)),
        out_specs=(tokens, tokens, P(("trow", "tcol"), "dp")),
        check_vma=False,
    )
```
